32 devices in a mesh: panel: 4 (over y, x), cap: 4 (over z), obs: 2 (over core).
Axes of the slice: x: 2, y: 2, z: 4, core: 2. Of those that a mesh axis runs over, the one named last changes fastest.
Arguments:
- surface: bfloat16 [2, 8192, 2560], P(None, ('panel', 'cap', 'obs')), may hold values from -6 to 6
- cap_of: int32 [8192], P(('panel', 'cap', 'obs')), may hold values from 0 to 31
- shift: int32 [64, 4], P(('panel', 'cap')), may hold values from 0 to 4
- amplitude: bfloat16 [3, 8192, 512], P(None, ('panel', 'cap'), 'obs'), may hold values from -0.09375 to 0.09375
Outputs:
- spectra: float32 [2, 256, 256], P('obs', ('panel', 'cap'))
The draws below stay inside these ranges and needn't reach their ends.
Inputs may be any that keep to these rules, and one draw needn't show every extreme that they name: `cap_of`: a panel with a value below 16 lies on that outflow cap; other panels lie on the lateral surface.
All inputs are finite; a program needn't handle non-finite values.
Results may differ from the reference program's by a relative error of at most 0.0011.
Values may be sent and summed in bfloat16 or wider, within the bound.
A program may use at most 64 MiB of HBM per device.

```python
import jax
import jax.numpy as jnp
from jax import lax

OBS = 512
BLK = 128
KMAX = 4
CAPS = 16
SEG = 512
NSEG = 7
HOP = 256
NBIN = 256
NT = 2048
NU = 2560
PANELS = 8192
N_OBS = 2


def plant(result, key, low, largest):
    index_at = [jax.random.randint(jax.random.fold_in(key, axis), (), 0, length) for axis, length in enumerate(result.shape)]
    widest = result.shape.index(max(result.shape))
    beside = index_at[:widest] + [(index_at[widest] + 1) % result.shape[widest]] + index_at[widest + 1:]
    return result.at[tuple(index_at)].set(low).at[tuple(beside)].set(largest)


def spiked(values, own_key, source, target, blocks, factor):
    def block_of(dim):
        return (jnp.arange(values.shape[dim]) // (values.shape[dim] // blocks)).reshape((-1,) + (1,) * (values.ndim - 1 - dim))

    one_side = jax.random.permutation(own_key, blocks)[block_of(target)]
    other_side = (block_of(target) + blocks // 2) % blocks
    return jnp.where((block_of(source) == one_side) | (block_of(source) == other_side), factor * values, values)


def shard_levels(stream_key, shape, shards, low, top_value):
    loudness, own = 1.0, jax.random.fold_in(stream_key, 6)
    for dim, shards_of in shards:
        steps = jnp.exp(jax.random.uniform(jax.random.fold_in(own, dim), (shards_of,), jnp.float32, low / len(shards), top_value / len(shards)))
        loudness = loudness * jnp.repeat(steps, shape[dim] // shards_of).reshape([-1 if axis == dim else 1 for axis in range(len(shape))])
    return loudness


def bell_draw(stream_key, shape, deviation, bound, shards=(), kind=jnp.bfloat16):
    values = deviation * jax.random.normal(stream_key, shape, jnp.float32)
    if shards:
        values = values * shard_levels(stream_key, shape, shards, -0.22, 0.18)
    return jnp.clip(values, -bound, bound).astype(kind)


def gaussian_with(own_key, shape, spread, reach, cuts, heavy, kind=jnp.bfloat16):
    values = spread * jax.random.normal(own_key, shape, jnp.float32)
    if cuts:
        values = values * shard_levels(own_key, shape, cuts, -0.22, 0.18)
    return jnp.clip(spiked(values, jax.random.fold_in(own_key, 3), *heavy), -reach, reach).astype(kind)


def setup_inputs(seed: int = 0) -> dict:
    key_list = jax.random.split(jax.random.key(seed), 5)
    return {
        "surface": bell_draw(key_list[0], (2, PANELS, NU), 1.0, 6.0, ((1, 32),)),
        "cap_of": plant(jax.random.randint(key_list[1], (PANELS,), 0, 2 * CAPS), jax.random.fold_in(key_list[1], 1), 0, (2 * CAPS) - 1).astype(jnp.int32),
        "shift": plant(jax.random.randint(key_list[2], (PANELS // BLK, OBS // BLK), 0, KMAX + 1), jax.random.fold_in(key_list[2], 1), 0, KMAX).astype(jnp.int32),
        "amplitude": gaussian_with(key_list[3], (3, PANELS, OBS), PANELS ** -0.5, 0.09375, ((1, 16), (2, 2)), (1, 2, 16, 2.0)),
    }


def make_series(surface, cap_of):
    weight = jnp.where(cap_of >= CAPS, jnp.float32(1.0), jnp.float32(1.0 / CAPS)).astype(jnp.float32)
    values = surface.astype(jnp.float32)
    after = jnp.concatenate([values[:, :, 1:], values[:, :, -1:]], axis=2)
    before = jnp.concatenate([values[:, :, :1], values[:, :, :-1]], axis=2)
    rates = (after - before) * 0.5
    stacked = jnp.stack([rates[0], rates[1], values[1]], axis=0) * weight[None, :, None]
    return stacked.astype(jnp.bfloat16)


def reference(surface, cap_of, shift, amplitude):
    series = make_series(surface, cap_of)
    ptiles = PANELS // BLK
    otiles = OBS // BLK
    tiles = series.reshape(3, ptiles, BLK, NU).transpose(1, 0, 2, 3)
    amp_tiles = amplitude.reshape(3, ptiles, BLK, otiles, BLK).transpose(1, 0, 2, 3, 4)

    def step(total, inputs):
        tile, krow, amp_tile = inputs
        windows = jax.vmap(lambda k: lax.dynamic_slice_in_dim(tile, ((KMAX - k) * BLK).astype(jnp.int32), NT, 2))(krow)
        part = jnp.einsum("cbqo,qcbn->qon", amp_tile.astype(jnp.float32), windows.astype(jnp.float32))
        return total + part, None

    start = jnp.zeros((otiles, BLK, NT), jnp.float32)
    signal = lax.scan(step, start, (tiles, shift, amp_tiles))[0].reshape(OBS, NT)
    steps_n = jnp.arange(SEG, dtype=jnp.float32)
    hann = 0.5 - 0.5 * jnp.cos(2.0 * jnp.pi * steps_n / SEG)
    pieces = jnp.stack([signal[:, j * HOP:j * HOP + SEG] for j in range(NSEG)], axis=1) * hann
    transform = jnp.fft.rfft(pieces, axis=2)[:, :, :NBIN]
    power = jnp.real(transform) ** 2 + jnp.imag(transform) ** 2
    spectra = jnp.mean(power, axis=1) / jnp.sum(hann * hann)
    return spectra.astype(jnp.float32).reshape(N_OBS, OBS // N_OBS, NBIN)
```

```python
import functools

import jax
import jax.numpy as jnp
import numpy as np
from jax import lax
from jax.experimental import pallas as pl
from jax.experimental.pallas import tpu as pltpu
from jax.sharding import PartitionSpec as P

BLK = 128
KMAX = 4
CAPS = 16
SEG = 512
NSEG = 7
HOP = 256
NBIN = 256
NT = 2048


def make_series(surface, cap_of):
    weight = jnp.where(cap_of >= CAPS, jnp.float32(1.0), jnp.float32(1.0 / CAPS))
    values = surface.astype(jnp.float32)
    after = jnp.concatenate([values[:, :, 1:], values[:, :, -1:]], axis=2)
    before = jnp.concatenate([values[:, :, :1], values[:, :, :-1]], axis=2)
    rates = (after - before) * 0.5
    stacked = jnp.stack([rates[0], rates[1], values[1]], axis=0) * weight[None, :, None]
    return stacked.astype(jnp.bfloat16)


def partial_signal(whole, amp, delays, base, length):
    terms, panels, samples = whole.shape
    ptiles = panels // BLK
    columns = amp.shape[2]
    otiles = columns // BLK
    tiles = whole.reshape(terms, ptiles, BLK, samples).transpose(1, 0, 2, 3)
    blocks = amp.reshape(terms, ptiles, BLK, otiles, BLK).transpose(1, 0, 2, 3, 4)

    def step(total, inputs):
        tile, delay_row, block = inputs
        windows = jax.vmap(
            lambda k: lax.dynamic_slice_in_dim(tile, base + (KMAX - k) * BLK, length, 2)
        )(delay_row)
        return (
            total
            + jnp.einsum("cbqo,qcbn->qon", block, windows, preferred_element_type=jnp.float32),
            None,
        )

    start = jnp.zeros((otiles, BLK, length), jnp.float32)
    total = lax.scan(step, start, (tiles, delays, blocks))[0]
    return total.reshape(columns, length)


def reduce_rows(partial_value):
    return lax.psum_scatter(partial_value, ("panel", "cap"), scatter_dimension=1, tiled=True)


def welch(signal):
    steps_n = jnp.arange(SEG, dtype=jnp.float32)
    hann = 0.5 - 0.5 * jnp.cos(2.0 * jnp.pi * steps_n / SEG)
    pieces = jnp.stack([signal[:, j * HOP : j * HOP + SEG] for j in range(NSEG)], axis=1) * hann
    index_n = jnp.arange(SEG, dtype=jnp.int32)
    index_f = jnp.arange(NBIN, dtype=jnp.int32)
    phase = (index_n[:, None] * index_f[None, :] % SEG).astype(jnp.float32) * (2.0 * jnp.pi / SEG)
    table = jnp.concatenate([jnp.cos(phase), -jnp.sin(phase)], axis=1)
    rows = signal.shape[0]
    spectrum = jnp.dot(
        pieces.reshape(rows * NSEG, SEG),
        table,
        precision=lax.Precision.HIGHEST,
        preferred_element_type=jnp.float32,
    )
    real_part = spectrum[:, :NBIN]
    imag_part = spectrum[:, NBIN:]
    power = (real_part * real_part + imag_part * imag_part).reshape(rows, NSEG, NBIN)
    return jnp.mean(power, axis=1) / jnp.sum(hann * hann)


def shards(surface, cap_of, shift, amplitude):
    local_series = make_series(surface, cap_of)
    whole = lax.all_gather(local_series, "obs", axis=1, tiled=True)
    otiles = amplitude.shape[2] // BLK
    delays = lax.dynamic_slice_in_dim(shift, lax.axis_index("obs") * otiles, otiles, 1)
    signal = partial_signal(whole, amplitude, delays, 0, NT)
    series_obs = reduce_rows(signal[None])[0]
    return welch(series_obs)[None]


MESH = pl.DeviceIdType.MESH
FULL = 32000.0
CHUNK = 512


def dft_tables():
    n = np.arange(SEG)
    hann = 0.5 - 0.5 * np.cos(2.0 * np.pi * n / SEG)
    phase = (n[:, None] * np.arange(NBIN)[None, :] % SEG) * (2.0 * np.pi / SEG)
    table = np.concatenate([np.cos(phase), -np.sin(phase)], axis=1) * hann[:, None]
    high = table.astype(jnp.bfloat16)
    low = (table - high.astype(np.float64)).astype(jnp.bfloat16)
    return high, low, float(np.sum(hann * hann)) * NSEG


def scale_of(largest):
    return jnp.exp2(jnp.ceil(jnp.log2(jnp.maximum(largest, 1e-30))))


def biggest(values):
    return jnp.max(jnp.abs(values), axis=(0, 1), keepdims=True)


def code(values, scale):
    return jnp.round(values * (FULL / scale)).astype(jnp.int32).astype(jnp.int16)


def decode(coded, scale):
    return coded.astype(jnp.float32) * (scale * (1.0 / FULL))


def fused(
    norm, shift_ref, surf_ref, cap_ref, amp_ref, high_ref, low_ref, out_ref,
    series, lhs, acc, other, amp_in,
    send_c, recv_c, send_a, recv_a, send_b, recv_b, send_z, recv_z,
    scale_out, scale_in, sem_amp, sem_data, sem_scale,
):
    panel, cap, obs = lax.axis_index("panel"), lax.axis_index("cap"), lax.axis_index("obs")
    y, x = panel // 2, panel % 2
    to_core = {"obs": 1 - obs}
    to_y = {"panel": (1 - y) * 2 + x}
    to_x = {"panel": y * 2 + 1 - x}
    caps = 4
    to_z = [{"cap": lax.rem(cap + d, caps)} for d in range(1, caps)]

    barrier = pltpu.get_barrier_semaphore()
    for target in [to_core, to_y, to_x] + to_z:
        pl.semaphore_signal(barrier, inc=1, device_id=target, device_id_type=MESH)
    pl.semaphore_wait(barrier, 6)

    def remote(src, dst, sems, number, target):
        return pltpu.make_async_remote_copy(
            src_ref=src, dst_ref=dst, send_sem=sems.at[0, number], recv_sem=sems.at[1, number],
            device_id=target, device_id_type=MESH,
        )

    half = 2 * BLK
    amp_copy = remote(amp_ref.at[:, pl.ds(pl.multiple_of((1 - obs) * half, half), half), :], amp_in, sem_amp, 0, to_core)
    amp_copy.start()

    weight = jnp.where(cap_ref[...] >= CAPS, 1.0, 1.0 / CAPS).astype(jnp.float32)
    for tile in range(2):
        rows = slice(tile * BLK, (tile + 1) * BLK)
        for term in range(2):
            v = surf_ref[term, rows, :]
            after = jnp.concatenate([v[:, 1:], v[:, -1:]], axis=1)
            before = jnp.concatenate([v[:, :1], v[:, :-1]], axis=1)
            rate = after - before
            for b in range(v.shape[1] // BLK):
                series[tile, b, term * BLK:(term + 1) * BLK, :] = rate[:, b * BLK:(b + 1) * BLK]
                if term == 1:
                    series[tile, b, 2 * BLK:3 * BLK, :] = v[:, b * BLK:(b + 1) * BLK]

    def fill(side, load):
        for tile in range(2):
            w = weight[:, tile * BLK:(tile + 1) * BLK]
            for part in range(2):
                for term in range(3):
                    block = load(term, tile, part).astype(jnp.float32).T
                    lhs[side * 2 + part, tile, :, term * BLK:(term + 1) * BLK] = (
                        block * (w * (1.0 if term == 2 else 0.5))
                    ).astype(jnp.bfloat16)

    fill(0, lambda term, tile, part: amp_ref[
        term, pl.ds(pl.multiple_of(obs * half + tile * BLK, BLK), BLK), part * BLK:(part + 1) * BLK])
    amp_copy.wait()
    fill(1, lambda term, tile, part: amp_in[term, tile * BLK:(tile + 1) * BLK, part * BLK:(part + 1) * BLK])

    def product(side, part, target, base):
        column = (obs if side == 0 else 1 - obs) * 2 + part
        largest = jnp.zeros((1, 1), jnp.float32)
        for i in range(NT // CHUNK):
            total = jnp.zeros((BLK, CHUNK), jnp.float32)
            for tile in range(2):
                begin = KMAX - shift_ref[obs * 2 + tile, column] + i * (CHUNK // BLK)
                window = jnp.concatenate([series[tile, begin + b] for b in range(CHUNK // BLK)], axis=1)
                total += jnp.dot(
                    lhs[side * 2 + part, tile], window,
                    preferred_element_type=jnp.float32,
                )
            target[base:base + BLK, i * CHUNK:(i + 1) * CHUNK] = total
            largest = jnp.maximum(largest, biggest(total))
        return largest

    pending = []

    def send(number, scale, src, dst, target):
        scale_out[number] = jnp.broadcast_to(scale, (8, 128))
        for copy in (
            remote(scale_out.at[number], scale_in.at[number], sem_scale, number, target),
            remote(src, dst, sem_data, number, target),
        ):
            copy.start()
            pending.append(copy)
        return pending[-2:]

    def take(number):
        return scale_in[number][0:1, 0:1]

    core_copies = []
    for part in range(2):
        scale = scale_of(product(1, part, other, 0))
        send_c[part] = code(other[...], scale)
        core_copies += send(part, scale, send_c.at[part], recv_c.at[part], to_core)
    for part in range(2):
        product(0, part, acc, part * BLK)
    for part in range(2):
        for copy in core_copies[2 * part:2 * part + 2]:
            copy.wait_recv()
        acc[part * BLK:(part + 1) * BLK, :] += decode(recv_c[part], take(part))

    mid = NT // 2
    quarter = BLK // 2
    early, late = slice(0, mid), slice(mid, NT)

    def at(row, size):
        return pl.ds(pl.multiple_of(row, quarter), size)

    give = acc[at((1 - y) * BLK, BLK), early]
    scale = scale_of(biggest(give))
    send_a[0] = code(give, scale)
    a_early = send(2, scale, send_a.at[0], recv_a.at[0], to_y)
    upper = acc[at((1 - x) * quarter, quarter), late]
    lower = acc[at(BLK + (1 - x) * quarter, quarter), late]
    scale = scale_of(jnp.maximum(biggest(upper), biggest(lower)))
    send_a[1, 0:quarter] = code(upper, scale)
    send_a[1, quarter:BLK] = code(lower, scale)
    a_late = send(3, scale, send_a.at[1], recv_a.at[1], to_x)

    for copy in a_early:
        copy.wait_recv()
    acc[at(y * BLK, BLK), early] += decode(recv_a[0], take(2))
    give = acc[at(y * BLK + (1 - x) * quarter, quarter), early]
    scale = scale_of(biggest(give))
    send_b[0] = code(give, scale)
    b_early = send(4, scale, send_b.at[0], recv_b.at[0], to_x)
    for copy in a_late:
        copy.wait_recv()
    for part in range(2):
        acc[at(part * BLK + x * quarter, quarter), late] += decode(
            recv_a[1, part * quarter:(part + 1) * quarter], take(3))
    give = acc[at((1 - y) * BLK + x * quarter, quarter), late]
    scale = scale_of(biggest(give))
    send_b[1] = code(give, scale)
    b_late = send(5, scale, send_b.at[1], recv_b.at[1], to_y)

    mine = at(y * BLK + x * quarter, quarter)
    for number, columns, copies in ((0, early, b_early), (1, late, b_late)):
        for copy in copies:
            copy.wait_recv()
        acc[mine, columns] += decode(recv_b[number], take(4 + number))

    rows = quarter // caps
    whole = acc[mine, :]
    scale = scale_of(biggest(whole))
    send_z[...] = code(whole, scale)
    z_copies = []
    for d in range(1, caps):
        place = pl.multiple_of(lax.rem(cap + d, caps) * rows, rows)
        z_copies.append(send(5 + d, scale, send_z.at[pl.ds(place, rows)], recv_z.at[d - 1], to_z[d - 1]))
    signal = acc[pl.ds(pl.multiple_of(y * BLK + x * quarter + cap * rows, rows), rows), :]
    for d in range(1, caps):
        for copy in z_copies[d - 1]:
            copy.wait_recv()
        signal += decode(recv_z[d - 1], take(5 + d))

    pieces = jnp.concatenate([signal[:, j * HOP:j * HOP + SEG] for j in range(NSEG)], axis=0)
    top = pieces.astype(jnp.bfloat16)
    rest = (pieces - top.astype(jnp.float32)).astype(jnp.bfloat16)
    dot = functools.partial(jnp.dot, preferred_element_type=jnp.float32)
    spectrum = dot(top, high_ref[...]) + (dot(rest, high_ref[...]) + dot(top, low_ref[...]))
    power = spectrum[:, :NBIN] ** 2 + spectrum[:, NBIN:] ** 2
    total = power[0:rows]
    for j in range(1, NSEG):
        total += power[j * rows:(j + 1) * rows]
    out_ref[...] = total * (1.0 / norm)

    for copy in pending:
        copy.wait_send()


def fused_shards(surface, cap_of, shift, amplitude):
    high, low, norm = dft_tables()
    vmem = pl.BlockSpec(memory_space=pltpu.VMEM)
    rows = BLK // 8
    out = pl.pallas_call(
        functools.partial(fused, norm),
        out_shape=jax.ShapeDtypeStruct((rows, NBIN), jnp.float32),
        in_specs=[pl.BlockSpec(memory_space=pltpu.SMEM)] + [vmem] * 5,
        out_specs=vmem,
        scratch_shapes=[
            pltpu.VMEM((2, surface.shape[2] // BLK, 3 * BLK, BLK), jnp.bfloat16),
            pltpu.VMEM((4, 2, BLK, 3 * BLK), jnp.bfloat16),
            pltpu.VMEM((2 * BLK, NT), jnp.float32),
            pltpu.VMEM((BLK, NT), jnp.float32),
            pltpu.VMEM((3, 2 * BLK, 2 * BLK), jnp.bfloat16),
            pltpu.VMEM((2, BLK, NT), jnp.int16),
            pltpu.VMEM((2, BLK, NT), jnp.int16),
            pltpu.VMEM((2, BLK, NT // 2), jnp.int16),
            pltpu.VMEM((2, BLK, NT // 2), jnp.int16),
            pltpu.VMEM((2, BLK // 2, NT // 2), jnp.int16),
            pltpu.VMEM((2, BLK // 2, NT // 2), jnp.int16),
            pltpu.VMEM((BLK // 2, NT), jnp.int16),
            pltpu.VMEM((3, rows, NT), jnp.int16),
            pltpu.VMEM((9, 8, 128), jnp.float32),
            pltpu.VMEM((9, 8, 128), jnp.float32),
            pltpu.SemaphoreType.DMA((2, 1)),
            pltpu.SemaphoreType.DMA((2, 9)),
            pltpu.SemaphoreType.DMA((2, 9)),
        ],
        compiler_params=pltpu.CompilerParams(
            collective_id=0, has_side_effects=True, vmem_limit_bytes=48 * 1024 * 1024
        ),
    )(shift, surface, cap_of.reshape(1, -1), amplitude, jnp.asarray(high), jnp.asarray(low))
    return out[None]


def suits(mesh):
    return mesh.shape["panel"] == 4 and mesh.shape["cap"] == 4 and mesh.shape["obs"] == 2


def solution(mesh):
    return jax.shard_map(
        fused_shards if suits(mesh) else shards,
        mesh=mesh,
        in_specs=(
            P(None, ("panel", "cap", "obs"), None),
            P(("panel", "cap", "obs")),
            P(("panel", "cap"), None),
            P(None, ("panel", "cap"), "obs"),
        ),
        out_specs=P("obs", ("panel", "cap"), None),
        check_vma=False,
    )
```

```python
import functools

import jax
import jax.numpy as jnp
import numpy as np
from jax import lax
from jax.experimental import pallas as pl
from jax.experimental.pallas import tpu as pltpu
from jax.sharding import PartitionSpec as P

BLK = 128
KMAX = 4
CAPS = 16
SEG = 512
NSEG = 7
HOP = 256
NBIN = 256
NT = 2048


def make_series(surface, cap_of):
    weight = jnp.where(cap_of >= CAPS, jnp.float32(1.0), jnp.float32(1.0 / CAPS))
    values = surface.astype(jnp.float32)
    after = jnp.concatenate([values[:, :, 1:], values[:, :, -1:]], axis=2)
    before = jnp.concatenate([values[:, :, :1], values[:, :, :-1]], axis=2)
    rates = (after - before) * 0.5
    stacked = jnp.stack([rates[0], rates[1], values[1]], axis=0) * weight[None, :, None]
    return stacked.astype(jnp.bfloat16)


def partial_signal(whole, amp, delays, base, length):
    terms, panels, samples = whole.shape
    ptiles = panels // BLK
    columns = amp.shape[2]
    otiles = columns // BLK
    tiles = whole.reshape(terms, ptiles, BLK, samples).transpose(1, 0, 2, 3)
    blocks = amp.reshape(terms, ptiles, BLK, otiles, BLK).transpose(1, 0, 2, 3, 4)

    def step(total, inputs):
        tile, delay_row, block = inputs
        windows = jax.vmap(
            lambda k: lax.dynamic_slice_in_dim(tile, base + (KMAX - k) * BLK, length, 2)
        )(delay_row)
        return (
            total
            + jnp.einsum("cbqo,qcbn->qon", block, windows, preferred_element_type=jnp.float32),
            None,
        )

    start = jnp.zeros((otiles, BLK, length), jnp.float32)
    total = lax.scan(step, start, (tiles, delays, blocks))[0]
    return total.reshape(columns, length)


def reduce_rows(partial_value):
    return lax.psum_scatter(partial_value, ("panel", "cap"), scatter_dimension=1, tiled=True)


def welch(signal):
    steps_n = jnp.arange(SEG, dtype=jnp.float32)
    hann = 0.5 - 0.5 * jnp.cos(2.0 * jnp.pi * steps_n / SEG)
    pieces = jnp.stack([signal[:, j * HOP : j * HOP + SEG] for j in range(NSEG)], axis=1) * hann
    index_n = jnp.arange(SEG, dtype=jnp.int32)
    index_f = jnp.arange(NBIN, dtype=jnp.int32)
    phase = (index_n[:, None] * index_f[None, :] % SEG).astype(jnp.float32) * (2.0 * jnp.pi / SEG)
    table = jnp.concatenate([jnp.cos(phase), -jnp.sin(phase)], axis=1)
    rows = signal.shape[0]
    spectrum = jnp.dot(
        pieces.reshape(rows * NSEG, SEG),
        table,
        precision=lax.Precision.HIGHEST,
        preferred_element_type=jnp.float32,
    )
    real_part = spectrum[:, :NBIN]
    imag_part = spectrum[:, NBIN:]
    power = (real_part * real_part + imag_part * imag_part).reshape(rows, NSEG, NBIN)
    return jnp.mean(power, axis=1) / jnp.sum(hann * hann)


def shards(surface, cap_of, shift, amplitude):
    local_series = make_series(surface, cap_of)
    whole = lax.all_gather(local_series, "obs", axis=1, tiled=True)
    otiles = amplitude.shape[2] // BLK
    delays = lax.dynamic_slice_in_dim(shift, lax.axis_index("obs") * otiles, otiles, 1)
    signal = partial_signal(whole, amplitude, delays, 0, NT)
    series_obs = reduce_rows(signal[None])[0]
    return welch(series_obs)[None]


MESH = pl.DeviceIdType.MESH
FULL = 32000.0
CHUNK = 512
CHIPS_Z = 4


def dft_tables():
    n = np.arange(SEG)
    hann = 0.5 - 0.5 * np.cos(2.0 * np.pi * n / SEG)
    phase = (n[:, None] * np.arange(NBIN)[None, :] % SEG) * (2.0 * np.pi / SEG)
    table = np.concatenate([np.cos(phase), -np.sin(phase)], axis=1) * hann[:, None]
    high = table.astype(jnp.bfloat16)
    low = (table - high.astype(np.float64)).astype(jnp.bfloat16)
    return high, low, float(np.sum(hann * hann)) * NSEG


def scale_of(largest):
    return jnp.exp2(jnp.ceil(jnp.log2(jnp.maximum(largest, 1e-30))))


def biggest(values):
    return jnp.max(jnp.abs(values), axis=(0, 1), keepdims=True)


def code(values, scale):
    return jnp.round(values * (FULL / scale)).astype(jnp.int32).astype(jnp.int16)


def decode(coded, scale):
    return coded.astype(jnp.float32) * (scale * (1.0 / FULL))


def fused(
    norm, shift_hbm, surf_hbm, cap_hbm, amp_hbm, high_hbm, low_hbm, out_ref,
    shift_ref, surf_ref, cap_ref, amp_own, high_ref, low_ref, amp_in,
    series, lhs, acc, other,
    send_c, recv_c, send_a, recv_a, send_b, recv_b, send_z, recv_z,
    scale_out, scale_in, sem_local, sem_amp, sem_data, sem_scale,
):
    panel, cap, obs = lax.axis_index("panel"), lax.axis_index("cap"), lax.axis_index("obs")
    y, x = panel // 2, panel % 2
    to_core = {"obs": 1 - obs}
    to_y = {"panel": (1 - y) * 2 + x}
    to_x = {"panel": y * 2 + 1 - x}
    to_z = [{"cap": lax.rem(cap + d, CHIPS_Z)} for d in range(1, CHIPS_Z)]

    barrier = pltpu.get_barrier_semaphore()
    for target in [to_core, to_y, to_x] + to_z:
        pl.semaphore_signal(barrier, inc=1, device_id=target, device_id_type=MESH)

    half = 2 * BLK
    own_half = amp_hbm.at[:, pl.ds(pl.multiple_of(obs * half, half), half), :]
    local = [
        pltpu.make_async_copy(src, dst, sem_local.at[i])
        for i, (src, dst) in enumerate((
            (surf_hbm, surf_ref), (cap_hbm, cap_ref), (own_half, amp_own),
            (shift_hbm, shift_ref), (high_hbm, high_ref), (low_hbm, low_ref),
        ))
    ]
    for copy in local:
        copy.start()
    pl.semaphore_wait(barrier, 6)

    def remote(src, dst, sems, number, target):
        return pltpu.make_async_remote_copy(
            src_ref=src, dst_ref=dst, send_sem=sems.at[0, number], recv_sem=sems.at[1, number],
            device_id=target, device_id_type=MESH,
        )

    amp_copy = remote(
        amp_hbm.at[:, pl.ds(pl.multiple_of((1 - obs) * half, half), half), :], amp_in, sem_amp, 0, to_core)
    amp_copy.start()

    local[0].wait()
    for tile in range(2):
        rows = slice(tile * BLK, (tile + 1) * BLK)
        for term in range(2):
            v = surf_ref[term, rows, :]
            after = jnp.concatenate([v[:, 1:], v[:, -1:]], axis=1)
            before = jnp.concatenate([v[:, :1], v[:, :-1]], axis=1)
            rate = after - before
            for b in range(v.shape[1] // BLK):
                series[tile, b, term * BLK:(term + 1) * BLK, :] = rate[:, b * BLK:(b + 1) * BLK]
                if term == 1:
                    series[tile, b, 2 * BLK:3 * BLK, :] = v[:, b * BLK:(b + 1) * BLK]

    for copy in local[1:]:
        copy.wait()
    weight = jnp.where(cap_ref[...] >= CAPS, 1.0, 1.0 / CAPS).astype(jnp.float32)

    def fill(side, amps):
        for tile in range(2):
            w = weight[:, tile * BLK:(tile + 1) * BLK]
            for part in range(2):
                for term in range(3):
                    block = amps[term, tile * BLK:(tile + 1) * BLK, part * BLK:(part + 1) * BLK]
                    lhs[side * 2 + part, tile, :, term * BLK:(term + 1) * BLK] = (
                        block.astype(jnp.float32).T * (w * (1.0 if term == 2 else 0.5))
                    ).astype(jnp.bfloat16)

    def product(side, chunk):
        largest = jnp.zeros((1, 1), jnp.float32)
        for part in range(2):
            column = (obs if side == 0 else 1 - obs) * 2 + part
            total = jnp.zeros((BLK, CHUNK), jnp.float32)
            for tile in range(2):
                begin = KMAX - shift_ref[obs * 2 + tile, column] + chunk * (CHUNK // BLK)
                window = jnp.concatenate([series[tile, begin + b] for b in range(CHUNK // BLK)], axis=1)
                total += jnp.dot(lhs[side * 2 + part, tile], window, preferred_element_type=jnp.float32)
            if side == 0:
                acc[part * BLK:(part + 1) * BLK, chunk * CHUNK:(chunk + 1) * CHUNK] = total
            else:
                other[part * BLK:(part + 1) * BLK, :] = total
                largest = jnp.maximum(largest, biggest(total))
        return largest

    sent = []

    def send(number, scale, src, dst, target):
        scale_out[number] = jnp.broadcast_to(scale, (8, 128))
        pair = (
            remote(scale_out.at[number], scale_in.at[number], sem_scale, number, target),
            remote(src, dst, sem_data, number, target),
        )
        for copy in pair:
            copy.start()
            sent.append(copy)
        return pair

    def arrived(pair):
        for copy in pair:
            copy.wait_recv()

    def take(number):
        return scale_in[number][0:1, 0:1]

    quarter = BLK // 2
    rows = quarter // CHIPS_Z
    coming = {}

    def at(row, size):
        return pl.ds(pl.multiple_of(row, rows), size)

    def span(chunk):
        return slice(chunk * CHUNK, (chunk + 1) * CHUNK)

    def to_other_core(chunk):
        scale = scale_of(product(1, chunk))
        send_c[chunk] = code(other[...], scale)
        coming["core", chunk] = send(6 * chunk, scale, send_c.at[chunk], recv_c.at[chunk], to_core)

    def first(chunk):
        arrived(coming["core", chunk])
        acc[:, span(chunk)] += decode(recv_c[chunk], take(6 * chunk))
        if chunk % 2 == 0:
            give = acc[at((1 - y) * BLK, BLK), span(chunk)]
        else:
            give = jnp.concatenate([
                acc[at((1 - x) * quarter, quarter), span(chunk)],
                acc[at(BLK + (1 - x) * quarter, quarter), span(chunk)],
            ], axis=0)
        scale = scale_of(biggest(give))
        send_a[chunk] = code(give, scale)
        coming["first", chunk] = send(
            6 * chunk + 1, scale, send_a.at[chunk], recv_a.at[chunk], to_y if chunk % 2 == 0 else to_x)

    def second(chunk):
        arrived(coming["first", chunk])
        scale = take(6 * chunk + 1)
        if chunk % 2 == 0:
            acc[at(y * BLK, BLK), span(chunk)] += decode(recv_a[chunk], scale)
            give = acc[at(y * BLK + (1 - x) * quarter, quarter), span(chunk)]
        else:
            for part in range(2):
                acc[at(part * BLK + x * quarter, quarter), span(chunk)] += decode(
                    recv_a[chunk, part * quarter:(part + 1) * quarter], scale)
            give = acc[at((1 - y) * BLK + x * quarter, quarter), span(chunk)]
        scale = scale_of(biggest(give))
        send_b[chunk] = code(give, scale)
        coming["second", chunk] = send(
            6 * chunk + 2, scale, send_b.at[chunk], recv_b.at[chunk], to_x if chunk % 2 == 0 else to_y)

    mine = y * BLK + x * quarter

    def third(chunk):
        arrived(coming["second", chunk])
        acc[at(mine, quarter), span(chunk)] += decode(recv_b[chunk], take(6 * chunk + 2))
        whole = acc[at(mine, quarter), span(chunk)]
        scale = scale_of(biggest(whole))
        send_z[chunk] = code(whole, scale)
        for d in range(1, CHIPS_Z):
            place = lax.rem(cap + d, CHIPS_Z) * rows
            coming["third", chunk, d] = send(
                6 * chunk + 2 + d, scale, send_z.at[chunk, at(place, rows)], recv_z.at[chunk, d - 1], to_z[d - 1])

    def last(chunk):
        signal = acc[at(mine + cap * rows, rows), span(chunk)]
        for d in range(1, CHIPS_Z):
            arrived(coming["third", chunk, d])
            signal += decode(recv_z[chunk, d - 1], take(6 * chunk + 2 + d))
        return signal

    fill(0, amp_own)
    amp_copy.wait()
    fill(1, amp_in)
    chunks = NT // CHUNK
    to_other_core(0)
    for chunk in range(chunks):
        if chunk + 1 < chunks:
            to_other_core(chunk + 1)
        product(0, chunk)
        first(chunk)
    for stage in (second, third):
        for chunk in range(chunks):
            stage(chunk)
    signal = jnp.concatenate([last(chunk) for chunk in range(chunks)], axis=1)

    pieces = jnp.concatenate([signal[:, j * HOP:j * HOP + SEG] for j in range(NSEG)], axis=0)
    top = pieces.astype(jnp.bfloat16)
    rest = (pieces - top.astype(jnp.float32)).astype(jnp.bfloat16)
    dot = functools.partial(jnp.dot, preferred_element_type=jnp.float32)
    spectrum = dot(top, high_ref[...]) + (dot(rest, high_ref[...]) + dot(top, low_ref[...]))
    power = spectrum[:, :NBIN] ** 2 + spectrum[:, NBIN:] ** 2
    total = power[0:rows]
    for j in range(1, NSEG):
        total += power[j * rows:(j + 1) * rows]
    out_ref[...] = total * (1.0 / norm)

    for copy in sent:
        copy.wait_send()


def fused_shards(surface, cap_of, shift, amplitude):
    high, low, norm = dft_tables()
    rows = BLK // 8
    chunks = NT // CHUNK
    caps = cap_of.reshape(1, -1)
    tables = jnp.asarray(high), jnp.asarray(low)
    pair = [
        pltpu.VMEM((chunks, size, CHUNK), jnp.int16)
        for size in (2 * BLK, 2 * BLK, BLK, BLK, BLK // 2, BLK // 2, BLK // 2)
    ]
    out = pl.pallas_call(
        functools.partial(fused, norm),
        out_shape=jax.ShapeDtypeStruct((rows, NBIN), jnp.float32),
        in_specs=[pl.BlockSpec(memory_space=pltpu.HBM)] * 6,
        out_specs=pl.BlockSpec(memory_space=pltpu.VMEM),
        scratch_shapes=[
            pltpu.SMEM(shift.shape, jnp.int32),
            pltpu.VMEM(surface.shape, surface.dtype),
            pltpu.VMEM(caps.shape, jnp.int32),
            pltpu.VMEM((3, 2 * BLK, 2 * BLK), jnp.bfloat16),
            pltpu.VMEM(high.shape, jnp.bfloat16),
            pltpu.VMEM(low.shape, jnp.bfloat16),
            pltpu.VMEM((3, 2 * BLK, 2 * BLK), jnp.bfloat16),
            pltpu.VMEM((2, surface.shape[2] // BLK, 3 * BLK, BLK), jnp.bfloat16),
            pltpu.VMEM((4, 2, BLK, 3 * BLK), jnp.bfloat16),
            pltpu.VMEM((2 * BLK, NT), jnp.float32),
            pltpu.VMEM((2 * BLK, CHUNK), jnp.float32),
            *pair,
            pltpu.VMEM((chunks, CHIPS_Z - 1, rows, CHUNK), jnp.int16),
            pltpu.VMEM((6 * chunks, 8, 128), jnp.float32),
            pltpu.VMEM((6 * chunks, 8, 128), jnp.float32),
            pltpu.SemaphoreType.DMA((6,)),
            pltpu.SemaphoreType.DMA((2, 1)),
            pltpu.SemaphoreType.DMA((2, 6 * chunks)),
            pltpu.SemaphoreType.DMA((2, 6 * chunks)),
        ],
        compiler_params=pltpu.CompilerParams(
            collective_id=0, has_side_effects=True, vmem_limit_bytes=63 * 1024 * 1024
        ),
    )(shift, surface, caps, amplitude, *tables)
    return out[None]


def suits(mesh):
    return mesh.shape["panel"] == 4 and mesh.shape["cap"] == 4 and mesh.shape["obs"] == 2


def solution(mesh):
    return jax.shard_map(
        fused_shards if suits(mesh) else shards,
        mesh=mesh,
        in_specs=(
            P(None, ("panel", "cap", "obs"), None),
            P(("panel", "cap", "obs")),
            P(("panel", "cap"), None),
            P(None, ("panel", "cap"), "obs"),
        ),
        out_specs=P("obs", ("panel", "cap"), None),
        check_vma=False,
    )
```
